256 devices in a mesh: expert: 32 (over z, y), loop: 8 (over x, core).
Axes of the slice: x: 4, y: 4, z: 8, core: 2. Of those that a mesh axis runs over, the one named last changes fastest.
Arguments:
- tokens: bfloat16 [4096, 5120], P('expert', 'loop'), may hold values from -6 to 6
- routes: int32 [4096, 6], P('expert'), may hold values from 0 to 31, all different within a row; in each aligned block of 128 rows (0 to 127, 128 to 255, ...) at most 32 rows name the same one
- route_weights: float32 [4096, 6], P('expert'), may hold values from 0.1 to 1
- gate_w: bfloat16 [32, 1536, 5120], P('expert', 'loop'), may hold values from -0.078125 to 0.078125
- up_w: bfloat16 [32, 1536, 5120], P('expert', 'loop'), may hold values from -0.078125 to 0.078125
- down_w: bfloat16 [32, 1536, 5120], P('expert', 'loop'), may hold values from -0.15625 to 0.15625
- shared_gate: bfloat16 [1536, 5120], P('loop'), may hold values from -0.078125 to 0.078125
- shared_up: bfloat16 [1536, 5120], P('loop'), may hold values from -0.078125 to 0.078125
- shared_down: bfloat16 [1536, 5120], P('loop'), may hold values from -0.15625 to 0.15625
Outputs:
- moe_out: bfloat16 [4096, 5120], P('expert', 'loop')
The draws below stay inside these ranges and needn't reach their ends.
Inputs may be any that keep to these rules, and one draw needn't show every extreme that they name: `routes`: within the rows of one device (aligned blocks of 128 rows) no expert is named by more than 32 rows; the 6 experts of a row differ.
All inputs are finite; a program needn't handle non-finite values.
Results may differ from the reference program's by a relative error of at most 0.02.
Values may be sent and summed in bfloat16 or wider, within the bound.
No kernel may reach another device: no remote copies, remote signals or barrier semaphores. Data moves between devices by JAX's collectives and lax.ppermute only.
A program may use at most 128 MiB of HBM per device.

```python
import math
import jax
import jax.numpy as jnp
import numpy as np
from jax import lax

D = 5120
FF = 1536
TOPK = 6
SH = 1536
TOK_DEV = 128
EXPERTS = 32
CAP = 32
TOKENS = 4096
N_EXPERT = 32
N_LOOP = 8


def steps_of(stream_key, dims, cuts, smallest, largest):
    gain = 1.0
    for dim, blocks in cuts:
        steps = jax.random.uniform(jax.random.fold_in(jax.random.fold_in(stream_key, 6), dim), (blocks,), jnp.float32, smallest / len(cuts), largest / len(cuts))
        gain = gain * jnp.repeat(jnp.exp(steps), dims[dim] // blocks).reshape((-1,) + (1,) * (len(dims) - 1 - dim))
    return gain


def shared_out(stream_key, own, number, rows, number_of, top, bound, skew):
    ranking = jax.random.permutation(stream_key, number_of)
    crowded, ordinary = load_shares(number_of, rows * top, bound, skew, True), load_shares(number_of, rows * top, bound, skew, False)
    places = jnp.arange(number_of)

    def named(sizes, rotation):
        used = int((sizes > 0).sum())
        fixed = max(1, used // 4)
        moved = fixed + (places - fixed + rotation * (used - fixed)) % max(1, number_of - fixed)
        return jnp.zeros((number_of,), jnp.int32).at[ranking[jnp.where(places < fixed, places, moved)]].set(jnp.asarray(sizes, jnp.int32))

    sizes = jnp.where(number % 4 == 0, named(crowded, number // 4), named(ordinary, number - number // 4 - 1))
    mixed = jax.random.permutation(jax.random.fold_in(own, 3), number_of)
    giver, taker = mixed[0:number_of // 2 * 2:2], mixed[1:number_of // 2 * 2:2]
    slack = jnp.minimum(sizes[giver] - 1, bound - sizes[taker]) // 2
    slack = jnp.where((giver == ranking[0]) | (taker == ranking[0]) | (sizes[taker] == 0), 0, jnp.maximum(slack, 0))
    moved = jax.random.randint(jax.random.fold_in(own, 4), (number_of // 2,), 0, 1 << 20) % (slack + 1)
    sizes = sizes.at[giver].add(-moved).at[taker].add(moved)
    items = jnp.searchsorted(jnp.cumsum(sizes), jnp.arange(rows * top), side="right").astype(jnp.int32)
    listing = items.reshape(top, rows).T
    listing = listing[jax.random.permutation(jax.random.fold_in(own, 1), rows)]
    rotation = jax.random.randint(jax.random.fold_in(own, 2), (rows, 1), 0, top)
    return jnp.take_along_axis(listing, (jnp.arange(top)[None, :] + rotation) % top, axis=1)


def load_shares(number_of, total, most, skew, full):
    weights = [(1 << 20) // math.isqrt(standing ** skew) + 1 for standing in range(1, number_of + 1)]
    largest = most if full else min(most, max(-(-total // number_of), total * weights[0] // sum(weights)))
    least = 1 if total - largest >= number_of - 1 else 0
    holding, surplus = [largest] + [least] * (number_of - 1), total - largest - least * (number_of - 1)
    while surplus > 0:
        movable = [i for i in range(1, number_of) if holding[i] < largest] or [i for i in range(1, number_of) if holding[i] < most]
        mass, budget = sum([weights[i] for i in movable]), surplus
        for i in movable:
            addition = min(most - holding[i], max(1, budget * weights[i] // mass), surplus)
            holding[i] = holding[i] + addition
            surplus = surplus - addition
    return np.array(holding)


def gaussian(stream_key, extent, spread, reach, split=(), held_as=jnp.bfloat16):
    array = jax.random.normal(stream_key, extent, jnp.float32) * spread
    if len(split) > 0:
        array = steps_of(stream_key, extent, split, -0.22, 0.18) * array
    return jnp.clip(array, min=-reach, max=reach).astype(held_as)


def setup_inputs(seed: int = 0) -> dict:
    key_list = jax.random.split(jax.random.key(seed), 10)
    tokens = gaussian(key_list[0], (TOKENS, D), 1.0, 6.0, ((0, 32), (1, 8)))
    routes_keys = jax.random.split(jax.random.fold_in(key_list[1], 1), TOKENS // TOK_DEV)
    routes_turns = jax.random.permutation(jax.random.fold_in(key_list[1], 3), TOKENS // TOK_DEV)
    routes = jax.vmap(lambda own, number: shared_out(jax.random.fold_in(key_list[1], 2), own, number, TOK_DEV, EXPERTS, TOPK, CAP, 2))(routes_keys, routes_turns).reshape((TOKENS, TOPK))
    route_weights = jnp.clip(0.1 + 0.9 * jax.random.uniform(key_list[2], (TOKENS, TOPK), jnp.float32) ** steps_of(key_list[2], (TOKENS, TOPK), ((0, 32),), -0.2, 0.2), 0.1, 1.0)
    gate_w = gaussian(key_list[3], (EXPERTS, FF, D), D ** -0.5, 0.078125, ((0, 32), (1, 8)))
    up_w = gaussian(key_list[4], (EXPERTS, FF, D), D ** -0.5, 0.078125, ((0, 32), (1, 8)))
    down_w = gaussian(key_list[5], (EXPERTS, FF, D), FF ** -0.5, 0.15625, ((0, 32), (1, 8)))
    shared_gate = gaussian(key_list[6], (SH, D), D ** -0.5, 0.078125, ((0, 8),))
    shared_up = gaussian(key_list[7], (SH, D), D ** -0.5, 0.078125, ((0, 8),))
    shared_down = gaussian(key_list[8], (SH, D), SH ** -0.5, 0.15625, ((0, 8),))
    return dict(tokens=tokens, routes=routes, route_weights=route_weights, gate_w=gate_w, up_w=up_w, down_w=down_w, shared_gate=shared_gate, shared_up=shared_up, shared_down=shared_down)


def expert_output(inputs_rows, w_gate, w_up, w_down):
    gate_act = lax.dot_general(inputs_rows, w_gate, (((1,), (1,)), ((), ())), preferred_element_type=jnp.float32)
    up_act = lax.dot_general(inputs_rows, w_up, (((1,), (1,)), ((), ())), preferred_element_type=jnp.float32)
    hidden = (jax.nn.silu(gate_act) * up_act).astype(jnp.bfloat16)
    slice_width = w_down.shape[0] // N_LOOP
    summed = jnp.zeros((inputs_rows.shape[0], w_down.shape[1]), jnp.float32)
    for block_index in range(N_LOOP):
        lower = block_index * slice_width
        partial_term = jnp.dot(hidden[:, lower:lower + slice_width], w_down[lower:lower + slice_width], preferred_element_type=jnp.float32)
        rounded = lax.optimization_barrier(partial_term.astype(jnp.bfloat16))
        summed = summed + rounded.astype(jnp.float32)
    return summed


def reference(tokens, routes, route_weights, gate_w, up_w, down_w, shared_gate, shared_up, shared_down):
    flat_routes = routes.reshape(N_EXPERT, TOK_DEV * TOPK)
    onehot = (flat_routes[:, :, None] == jnp.arange(EXPERTS, dtype=jnp.int32)[None, None, :]).astype(jnp.int32)
    before = jnp.cumsum(onehot, axis=1) - onehot
    position = jnp.sum(before * onehot, axis=2).astype(jnp.int32)
    group_ids = jnp.arange(N_EXPERT, dtype=jnp.int32)[:, None]
    token_ids = group_ids * TOK_DEV + jnp.arange(TOK_DEV * TOPK, dtype=jnp.int32)[None, :] // TOPK
    slot_rows = (group_ids * CAP + position).astype(jnp.int32)
    row_table = jnp.full((EXPERTS, N_EXPERT * CAP), TOKENS, jnp.int32)
    row_table = row_table.at[flat_routes, slot_rows].set(token_ids)
    padded = jnp.concatenate([tokens, jnp.zeros((1, D), tokens.dtype)], axis=0)

    def one_expert(operands):
        table_row, w_gate, w_up, w_down = operands
        return expert_output(padded[table_row], w_gate, w_up, w_down).astype(jnp.bfloat16)

    expert_outputs = lax.map(one_expert, (row_table, gate_w, up_w, down_w))
    slot_flat = slot_rows.reshape(TOKENS, TOPK)
    routed = jnp.zeros((TOKENS, D), jnp.float32)
    for slot_k in range(TOPK):
        picked = expert_outputs[routes[:, slot_k], slot_flat[:, slot_k]].astype(jnp.float32)
        routed = routed + route_weights[:, slot_k][:, None] * picked
    shared = expert_output(tokens, shared_gate, shared_up, shared_down)
    return (routed + shared).astype(jnp.bfloat16)
```

```python
import jax
import jax.numpy as jnp
from jax import lax
from jax.sharding import PartitionSpec as P

CHIPS = 4
BF16 = jnp.bfloat16
F32 = jnp.float32


def swap_cores(value):
    return lax.ppermute(value, "loop", [(i, i ^ 1) for i in range(2 * CHIPS)])


def shift_chips(value, step):
    pairs = [
        (2 * chip + core, 2 * ((chip + step) % CHIPS) + core)
        for chip in range(CHIPS)
        for core in range(2)
    ]
    return lax.ppermute(value, "loop", pairs)


def gather_chips(block):
    half = block.shape[0] // 2
    first, second = block[:half], block[half:]
    first_left, first_right = shift_chips(first, 1), shift_chips(first, -1)
    second_left, second_right = shift_chips(second, 1), shift_chips(second, -1)
    first_far, second_far = shift_chips(first_left, 1), shift_chips(second_right, -1)
    return (
        [first, first_left, first_far, first_right],
        [second, second_left, second_far, second_right],
    )


def project_rows(rows, weight):
    return lax.dot_general(rows, weight, (((1,), (1,)), ((), ())), preferred_element_type=F32)


def dot(left, right):
    return jnp.dot(left, right, preferred_element_type=F32)


def pick(chip, step, array, width):
    return lax.dynamic_slice_in_dim(array, ((chip - step) & (CHIPS - 1)) * width, width, axis=1)


def hidden_of(blocks, gates, ups, chip):
    width = blocks[0].shape[1]
    out = []
    for gate, up in zip(gates, ups):
        gate_act = sum(project_rows(b, pick(chip, k, gate, width)) for k, b in enumerate(blocks))
        up_act = sum(project_rows(b, pick(chip, k, up, width)) for k, b in enumerate(blocks))
        out.append((jax.nn.silu(gate_act) * up_act).astype(BF16))
    return jnp.concatenate(out, axis=1)


def local(tokens, routes, route_weights, gate_w, up_w, down_w, shared_gate, shared_up, shared_down):
    tok_rows, width = tokens.shape
    experts = lax.axis_size("expert")
    half_cap = tok_rows * routes.shape[1] * 4 // (3 * experts) // 2
    place = lax.axis_index("loop")
    chip, core = place >> 1, place & 1
    first_core = core == 0

    def both(own):
        other = swap_cores(own)
        return jnp.where(
            first_core,
            jnp.concatenate([own, other], axis=1),
            jnp.concatenate([other, own], axis=1),
        )

    chip_tokens = both(tokens)
    chip_width = 2 * width

    own_down = down_w[0]
    down_own = [pick(chip, 0, own_down, chip_width)] + [
        shift_chips(pick(chip, -k, own_down, chip_width), k) for k in range(1, CHIPS)
    ]
    down_other = [swap_cores(part) for part in down_own]
    down_all = jnp.concatenate([p for pair in zip(down_own, down_other) for p in pair], axis=0)
    gates = [gate_w[0], swap_cores(gate_w[0])]
    ups = [up_w[0], swap_cores(up_w[0])]
    shared_gates = [shared_gate, swap_cores(shared_gate)]
    shared_ups = [shared_up, swap_cores(shared_up)]
    shared_downs = [shared_down, swap_cores(shared_down)]

    ids = jnp.arange(experts, dtype=jnp.int32)
    equal = routes.T[:, None, :] == ids[None, :, None]
    member = jnp.any(equal, axis=0)
    weight = jnp.sum(jnp.where(equal, route_weights.T[:, None, :], 0.0), axis=0)
    row = lax.broadcasted_iota(jnp.int32, (tok_rows, tok_rows), 0)
    col = lax.broadcasted_iota(jnp.int32, (tok_rows, tok_rows), 1)
    before = dot(member.astype(BF16), (row < col).astype(BF16)).astype(jnp.int32)
    slots = jnp.arange(half_cap, dtype=jnp.int32) + core * half_cap
    hit = member[:, None, :] & (before[:, None, :] == slots[None, :, None])
    selector = hit.astype(BF16).reshape(experts * half_cap, tok_rows)
    combine = jnp.where(hit, weight[:, None, :], 0.0).reshape(experts * half_cap, tok_rows)
    combine_high = combine.astype(BF16)
    combine_low = (combine - combine_high.astype(F32)).astype(BF16)

    outgoing = dot(selector, chip_tokens).astype(BF16)
    outgoing = outgoing.reshape(experts, half_cap, chip_width)
    incoming = lax.all_to_all(outgoing, "expert", split_axis=0, concat_axis=0, tiled=True)
    rows = incoming.reshape(experts * half_cap, chip_width)

    half_tok = tok_rows // 2
    my_tokens = lax.dynamic_slice_in_dim(chip_tokens, core * half_tok, half_tok, axis=0)
    shared_blocks = [my_tokens] + [shift_chips(my_tokens, k) for k in range(1, CHIPS)]
    shared_hidden = hidden_of(shared_blocks, shared_gates, shared_ups, chip)
    unit = shared_down.shape[0]
    shared_part = (
        dot(shared_hidden[:, :unit], shared_downs[0]) + dot(shared_hidden[:, unit:], shared_downs[1])
    ).astype(BF16)
    shared_sum = pick(chip, 0, shared_part, chip_width).astype(F32)
    for k in range(1, CHIPS):
        shared_sum = shared_sum + shift_chips(
            pick(chip, -k, shared_part, chip_width), k
        ).astype(F32)

    halves = gather_chips(rows)
    results = []
    for blocks in halves:
        hidden = hidden_of(blocks, gates, ups, chip)
        hiddens = [hidden] + [shift_chips(hidden, k) for k in range(1, CHIPS)]
        results.append(dot(jnp.concatenate(hiddens, axis=1), down_all).astype(BF16))
    result = jnp.concatenate(results, axis=0).reshape(experts, half_cap, chip_width)
    returned = lax.all_to_all(result, "expert", split_axis=0, concat_axis=0, tiled=True)
    returned = returned.reshape(experts * half_cap, chip_width)
    contract = (((0,), (0,)), ((), ()))
    routed = lax.dot_general(combine_high, returned, contract, preferred_element_type=F32)
    routed = routed + lax.dot_general(combine_low, returned, contract, preferred_element_type=F32)
    zeros = jnp.zeros((half_tok, chip_width), F32)
    placed = jnp.where(
        first_core,
        jnp.concatenate([shared_sum, zeros], axis=0),
        jnp.concatenate([zeros, shared_sum], axis=0),
    )
    total = routed + placed
    mine = lax.dynamic_slice_in_dim(total, core * width, width, axis=1)
    theirs = lax.dynamic_slice_in_dim(total, (1 - core) * width, width, axis=1)
    return (mine + swap_cores(theirs)).astype(BF16)


def solution(mesh):
    placed = (
        P("expert", "loop"),
        P("expert", None),
        P("expert", None),
        P("expert", "loop", None),
        P("expert", "loop", None),
        P("expert", "loop", None),
        P("loop", None),
        P("loop", None),
        P("loop", None),
    )
    return jax.shard_map(
        local, mesh=mesh, in_specs=placed, out_specs=P("expert", "loop"), check_vma=False
    )
```

```python
import jax
import jax.numpy as jnp
from jax import lax
from jax.experimental import pallas as pl
from jax.experimental.pallas import tpu as pltpu
from jax.sharding import PartitionSpec as P

CHIPS = 4
BF16 = jnp.bfloat16
F32 = jnp.float32


def swap_cores(value):
    return lax.ppermute(value, "loop", [(i, i ^ 1) for i in range(2 * CHIPS)])


def shift_chips(value, step):
    pairs = [
        (2 * chip + core, 2 * ((chip + step) % CHIPS) + core)
        for chip in range(CHIPS)
        for core in range(2)
    ]
    return lax.ppermute(value, "loop", pairs)


def dot(left, right):
    return jnp.dot(left, right, preferred_element_type=F32)


def project_rows(rows, weight):
    return lax.dot_general(rows, weight, (((1,), (1,)), ((), ())), preferred_element_type=F32)


def pick(chip, step, array, width):
    return lax.dynamic_slice_in_dim(array, ((chip - step) & (CHIPS - 1)) * width, width, axis=1)


def hidden_of(act):
    unit = act.shape[1] // 2
    return (jax.nn.silu(act[:, :unit]) * act[:, unit:]).astype(BF16)


def roll_kernel(chip_ref, *refs):
    out = refs[-1]
    unit = refs[0].shape[0]
    for i, ref in enumerate(refs[:-1]):
        out[0, i * unit : (i + 1) * unit, :] = ref[...]


def roll_features(chip, weights, width):
    unit = weights[0].shape[0]
    rows = unit * len(weights)
    return pl.pallas_call(
        roll_kernel,
        out_shape=jax.ShapeDtypeStruct((CHIPS, rows, width), BF16),
        grid_spec=pltpu.PrefetchScalarGridSpec(
            num_scalar_prefetch=1,
            grid=(CHIPS,),
            in_specs=[pl.BlockSpec((unit, width), lambda k, c: (0, (c[0] - k) & (CHIPS - 1)))]
            * len(weights),
            out_specs=pl.BlockSpec((1, rows, width), lambda k, c: (k, 0, 0)),
        ),
        compiler_params=pltpu.CompilerParams(vmem_limit_bytes=24 << 20),
    )(chip.reshape(1), *weights)


def local(tokens, routes, route_weights, gate_w, up_w, down_w, shared_gate, shared_up, shared_down):
    tok_rows, width = tokens.shape
    experts = lax.axis_size("expert")
    half_cap = tok_rows * routes.shape[1] * 4 // (3 * experts) // 2
    place = lax.axis_index("loop")
    chip, core = place >> 1, place & 1
    first_core = core == 0
    chip_width = 2 * width
    steps = (1, 3, 2)

    other_tokens = swap_cores(tokens)
    down_own = [pick(chip, 0, down_w[0], chip_width)] + [
        shift_chips(pick(chip, -k, down_w[0], chip_width), k) for k in steps
    ]
    chip_tokens = jnp.where(
        first_core,
        jnp.concatenate([tokens, other_tokens], axis=1),
        jnp.concatenate([other_tokens, tokens], axis=1),
    )

    ids = jnp.arange(experts, dtype=jnp.int32)
    equal = routes.T[:, None, :] == ids[None, :, None]
    member = jnp.any(equal, axis=0)
    weight = jnp.sum(jnp.where(equal, route_weights.T[:, None, :], 0.0), axis=0)
    row = lax.broadcasted_iota(jnp.int32, (tok_rows, tok_rows), 0)
    col = lax.broadcasted_iota(jnp.int32, (tok_rows, tok_rows), 1)
    before = dot(member.astype(BF16), (row < col).astype(BF16)).astype(jnp.int32)
    slots = jnp.arange(half_cap, dtype=jnp.int32) + core * half_cap
    hit = member[:, None, :] & (before[:, None, :] == slots[None, :, None])
    selector = hit.astype(BF16).reshape(experts * half_cap, tok_rows)
    outgoing = dot(selector, chip_tokens).astype(BF16)

    def exchange(value):
        value = value.reshape(experts, half_cap, chip_width)
        value = lax.all_to_all(value, "expert", split_axis=0, concat_axis=0, tiled=True)
        return value.reshape(experts * half_cap, chip_width)

    rows = exchange(outgoing)

    gate_own, up_own, sent_tokens, down_own, _ = lax.optimization_barrier(
        (gate_w[0], up_w[0], chip_tokens, down_own, outgoing)
    )
    down_four = jnp.stack(down_own)
    down_all = jnp.stack([down_four, swap_cores(down_four)], axis=1).reshape(-1, chip_width)
    gate_other, up_other = swap_cores(gate_own), swap_cores(up_own)
    weights = roll_features(chip, [gate_own, gate_other, up_own, up_other], chip_width)
    token_blocks = [sent_tokens] + [shift_chips(sent_tokens, k) for k in steps]
    rows, weights, down_all, token_blocks = lax.optimization_barrier(
        (rows, weights, down_all, token_blocks)
    )

    cut = rows.shape[0] * 3 // 4
    pieces = [rows[:cut], rows[cut:]]
    gathered = []
    for piece in pieces:
        if gathered:
            gathered[-1], piece = lax.optimization_barrier((gathered[-1], piece))
        gathered.append((piece, shift_chips(piece, 1), shift_chips(piece, -1)))

    def project_in(piece, left, right):
        half = piece.shape[0] // 2
        far = [shift_chips(left[:half], 1), shift_chips(right[half:], -1)]
        act = project_rows(piece, weights[0]) + project_rows(left, weights[1])
        act = act + project_rows(right, weights[3])
        act = act + jnp.concatenate([project_rows(part, weights[2]) for part in far], axis=0)
        hidden = hidden_of(act)
        hiddens = [hidden] + [shift_chips(hidden, k) for k in steps]
        return dot(jnp.concatenate(hiddens, axis=1), down_all).astype(BF16)

    result = jnp.concatenate([project_in(*piece) for piece in gathered], axis=0)

    whole = jnp.zeros((tok_rows, CHIPS * chip_width), BF16)
    for block, k in zip(token_blocks, (0,) + steps):
        at = ((chip - k) & (CHIPS - 1)) * chip_width
        whole = lax.dynamic_update_slice_in_dim(whole, block, at, axis=1)
    shared_hidden = (
        jax.nn.silu(project_rows(whole, shared_gate)) * project_rows(whole, shared_up)
    ).astype(BF16)
    shared_part = dot(shared_hidden, shared_down).astype(BF16)
    result, shared_part = lax.optimization_barrier((result, shared_part))
    returned = exchange(result)

    shared = pick(chip, 0, shared_part, chip_width).astype(F32)
    for k in steps:
        shared = shared + shift_chips(pick(chip, -k, shared_part, chip_width), k).astype(F32)
    combine = jnp.where(hit, weight[:, None, :], 0.0).reshape(experts * half_cap, tok_rows)
    high = combine.astype(BF16)
    low = (combine - high.astype(F32)).astype(BF16)
    contract = (((0,), (0,)), ((), ()))
    total = shared + lax.dot_general(high, returned, contract, preferred_element_type=F32)
    total = total + lax.dot_general(low, returned, contract, preferred_element_type=F32)
    mine = lax.dynamic_slice_in_dim(total, core * width, width, axis=1)
    theirs = lax.dynamic_slice_in_dim(total, (1 - core) * width, width, axis=1)
    return (mine + swap_cores(theirs)).astype(BF16)


def solution(mesh):
    placed = (
        P("expert", "loop"),
        P("expert", None),
        P("expert", None),
        P("expert", "loop", None),
        P("expert", "loop", None),
        P("expert", "loop", None),
        P("loop", None),
        P("loop", None),
        P("loop", None),
    )
    return jax.shard_map(
        local, mesh=mesh, in_specs=placed, out_specs=P("expert", "loop"), check_vma=False
    )
```

```python
import jax
import jax.numpy as jnp
from jax import lax
from jax.experimental import pallas as pl
from jax.experimental.pallas import tpu as pltpu
from jax.sharding import PartitionSpec as P

CHIPS = 4
BF16 = jnp.bfloat16
F32 = jnp.float32


def swap_cores(value):
    return lax.ppermute(value, "loop", [(i, i ^ 1) for i in range(2 * CHIPS)])


def shift_chips(value, step):
    pairs = [
        (2 * chip + core, 2 * ((chip + step) % CHIPS) + core)
        for chip in range(CHIPS)
        for core in range(2)
    ]
    return lax.ppermute(value, "loop", pairs)


def dot(left, right):
    return jnp.dot(left, right, preferred_element_type=F32)


def project_rows(rows, weight):
    return lax.dot_general(rows, weight, (((1,), (1,)), ((), ())), preferred_element_type=F32)


def pick(chip, step, array, width):
    return lax.dynamic_slice_in_dim(array, ((chip - step) & (CHIPS - 1)) * width, width, axis=1)


def hidden_of(act):
    unit = act.shape[1] // 2
    return (jax.nn.silu(act[:, :unit]) * act[:, unit:]).astype(BF16)


def select_kernel(core_ref, tokens, other, chosen, out, half):
    first = core_ref[0] == 0
    whole = jnp.where(
        first,
        jnp.concatenate([tokens[...], other[...]], axis=1),
        jnp.concatenate([other[...], tokens[...]], axis=1),
    )
    out[...] = dot(chosen[...], whole).astype(BF16)
    rows = half.shape[0]
    half[...] = jnp.where(first, whole[:rows], whole[rows:])


def select_rows(core, tokens, other, chosen):
    rows, width = tokens.shape
    arrays = (tokens, other, chosen)
    shapes = [(chosen.shape[0], 2 * width), (rows // 2, 2 * width)]
    return pl.pallas_call(
        select_kernel,
        out_shape=[jax.ShapeDtypeStruct(shape, BF16) for shape in shapes],
        grid_spec=pltpu.PrefetchScalarGridSpec(
            num_scalar_prefetch=1,
            grid=(1,),
            in_specs=[pl.BlockSpec(array.shape, lambda k, c: (0, 0)) for array in arrays],
            out_specs=[pl.BlockSpec(shape, lambda k, c: (0, 0)) for shape in shapes],
        ),
        compiler_params=pltpu.CompilerParams(vmem_limit_bytes=24 << 20),
    )(core.reshape(1), *arrays)


def roll_kernel(chip_ref, *refs):
    out = refs[-1]
    unit = refs[0].shape[0]
    for i, ref in enumerate(refs[:-1]):
        out[0, i * unit : (i + 1) * unit, :] = ref[...]


def roll_features(chip, weights, width):
    unit = weights[0].shape[0]
    rows = unit * len(weights)
    return pl.pallas_call(
        roll_kernel,
        out_shape=jax.ShapeDtypeStruct((CHIPS, rows, width), BF16),
        grid_spec=pltpu.PrefetchScalarGridSpec(
            num_scalar_prefetch=1,
            grid=(CHIPS,),
            in_specs=[pl.BlockSpec((unit, width), lambda k, c: (0, (c[0] - k) & (CHIPS - 1)))]
            * len(weights),
            out_specs=pl.BlockSpec((1, rows, width), lambda k, c: (k, 0, 0)),
        ),
        compiler_params=pltpu.CompilerParams(vmem_limit_bytes=24 << 20),
    )(chip.reshape(1), *weights)


def join_kernel(*refs):
    out = refs[-1]
    unit = refs[0].shape[0]
    for i, ref in enumerate(refs[:-1]):
        out[i * unit : (i + 1) * unit, :] = ref[...]


def join_rows(pieces):
    unit, width = pieces[0].shape
    tile = width // 2
    return pl.pallas_call(
        join_kernel,
        out_shape=jax.ShapeDtypeStruct((unit * len(pieces), width), BF16),
        grid=(2,),
        in_specs=[pl.BlockSpec((unit, tile), lambda n: (0, n))] * len(pieces),
        out_specs=pl.BlockSpec((unit * len(pieces), tile), lambda n: (0, n)),
        compiler_params=pltpu.CompilerParams(vmem_limit_bytes=24 << 20),
    )(*pieces)


def act_of(gate, up):
    return (gate / (1.0 + jnp.exp(-gate)) * up).astype(BF16)


def shared_kernel(where_ref, mine, other, gate, up, down, *refs):
    keep, give, gate_acc, up_acc, hidden = refs
    step = pl.program_id(0)
    rows = mine.shape[0] // CHIPS

    @pl.when(step < CHIPS)
    def _():
        at = pl.ds(pl.multiple_of(step * rows, rows), rows)
        block = jnp.concatenate([mine[at, :], other[at, :]], axis=0)
        first = step == 0
        gate_term, up_term = project_rows(block, gate[...]), project_rows(block, up[...])
        gate_acc[...] = jnp.where(first, gate_term, gate_acc[...] + gate_term)
        up_acc[...] = jnp.where(first, up_term, up_acc[...] + up_term)

    @pl.when(step == CHIPS - 1)
    def _():
        hidden[...] = act_of(gate_acc[...], up_acc[...])

    @pl.when(step >= CHIPS)
    def _():
        at = pl.ds(pl.multiple_of((step - CHIPS) * rows, rows), rows)
        term = dot(hidden[...], down[...]).astype(BF16)
        keep[at, :] = term[:rows]
        give[at, :] = term[rows:]


def shared_terms(where, mine, other, gate, up, down):
    unit = gate.shape[0]
    rows, width = mine.shape[0] // CHIPS * 2, mine.shape[1]

    def near(k):
        return k ^ (k >> 1)

    whole = pl.BlockSpec(mine.shape, lambda k, w: (0, 0))
    into = pl.BlockSpec(
        (unit, width), lambda k, w: (0, (w[0] - near(jnp.minimum(k, CHIPS - 1))) & (CHIPS - 1))
    )
    out_of = pl.BlockSpec(
        (unit, width), lambda k, w: (0, (w[0] + near(jnp.maximum(k - CHIPS, 0))) & (CHIPS - 1))
    )
    return pl.pallas_call(
        shared_kernel,
        out_shape=[jax.ShapeDtypeStruct(mine.shape, BF16)] * 2,
        grid_spec=pltpu.PrefetchScalarGridSpec(
            num_scalar_prefetch=1,
            grid=(2 * CHIPS,),
            in_specs=[whole, whole, into, into, out_of],
            out_specs=[whole] * 2,
            scratch_shapes=[
                pltpu.VMEM((rows, unit), F32),
                pltpu.VMEM((rows, unit), F32),
                pltpu.VMEM((rows, unit), BF16),
            ],
        ),
        compiler_params=pltpu.CompilerParams(vmem_limit_bytes=24 << 20),
    )(where, mine, other, gate, up, down)


def combine_kernel(where_ref, high, low, returned, *refs):
    shared, (mine, theirs) = refs[:CHIPS], refs[CHIPS:]
    contract = (((0,), (0,)), ((), ()))
    part = sum(ref[...].astype(F32) for ref in shared)
    none = jnp.zeros_like(part)
    total = jnp.where(
        where_ref[1] == 0,
        jnp.concatenate([part, none], axis=0),
        jnp.concatenate([none, part], axis=0),
    )
    for weight in (high, low):
        total = total + lax.dot_general(
            weight[...], returned[...], contract, preferred_element_type=F32
        )
    width = mine.shape[1]
    first = where_ref[1] == 0
    mine[...] = jnp.where(first, total[:, :width], total[:, width:])
    theirs[...] = jnp.where(first, total[:, width:], total[:, :width])


def combine(where, high, low, returned, shared):
    rows, width = high.shape[1], returned.shape[1]
    half = jax.ShapeDtypeStruct((rows, width // 2), F32)
    arrays = (high, low, returned, *shared)
    return pl.pallas_call(
        combine_kernel,
        out_shape=[half, half],
        grid_spec=pltpu.PrefetchScalarGridSpec(
            num_scalar_prefetch=1,
            grid=(1,),
            in_specs=[pl.BlockSpec(array.shape, lambda k, w: (0, 0)) for array in arrays],
            out_specs=[pl.BlockSpec(half.shape, lambda k, w: (0, 0))] * 2,
        ),
        compiler_params=pltpu.CompilerParams(vmem_limit_bytes=24 << 20),
    )(where, *arrays)


def local(tokens, routes, route_weights, gate_w, up_w, down_w, shared_gate, shared_up, shared_down):
    tok_rows, width = tokens.shape
    experts = lax.axis_size("expert")
    half_cap = tok_rows * routes.shape[1] * 4 // (3 * experts) // 2
    place = lax.axis_index("loop")
    chip, core = place >> 1, place & 1
    chip_width = 2 * width
    steps = (1, 3, 2)

    other_tokens = swap_cores(tokens)
    ids = jnp.arange(experts, dtype=jnp.int32)
    equal = routes.T[:, None, :] == ids[None, :, None]
    member = jnp.any(equal, axis=0)
    weight = jnp.sum(jnp.where(equal, route_weights.T[:, None, :], 0.0), axis=0)
    row = lax.broadcasted_iota(jnp.int32, (tok_rows, tok_rows), 0)
    col = lax.broadcasted_iota(jnp.int32, (tok_rows, tok_rows), 1)
    before = dot(member.astype(BF16), (row < col).astype(BF16)).astype(jnp.int32)
    slots = jnp.arange(half_cap, dtype=jnp.int32) + core * half_cap
    hit = member[:, None, :] & (before[:, None, :] == slots[None, :, None])
    selector = hit.astype(BF16).reshape(experts * half_cap, tok_rows)
    outgoing, sent_tokens = select_rows(core, tokens, other_tokens, selector)

    def exchange(value):
        value = value.reshape(experts, half_cap, chip_width)
        value = lax.all_to_all(value, "expert", split_axis=0, concat_axis=0, tiled=True)
        return value.reshape(experts * half_cap, chip_width)

    rows = exchange(outgoing)

    gate_own, up_own, down_mine, sent_tokens, _ = lax.optimization_barrier(
        (gate_w[0], up_w[0], down_w[0], sent_tokens, outgoing)
    )
    down_own = [pick(chip, 0, down_mine, chip_width)] + [
        shift_chips(pick(chip, -k, down_mine, chip_width), k) for k in steps
    ]
    gate_other, up_other = swap_cores(gate_own), swap_cores(up_own)
    sent_tokens, gate_other, up_other = lax.optimization_barrier(
        (sent_tokens, gate_other, up_other)
    )
    weights = roll_features(chip, [gate_own, gate_other, up_own, up_other], chip_width)
    token_blocks = [sent_tokens] + [shift_chips(sent_tokens, k) for k in steps]
    down_own, token_blocks[1:3], weights = lax.optimization_barrier(
        (down_own, token_blocks[1:3], weights)
    )
    down_four = join_rows(down_own)
    down_other = swap_cores(down_four)
    rows, weights, down_own, down_other, token_blocks = lax.optimization_barrier(
        (rows, weights, down_own, down_other, token_blocks)
    )
    down_other = jnp.split(down_other, CHIPS)
    down_all = join_rows([part for pair in zip(down_own, down_other) for part in pair])

    cut = rows.shape[0] // 2
    pieces = [rows[:cut], rows[cut:]]
    sides = [(shift_chips(piece, 1), shift_chips(piece, -1)) for piece in pieces]
    acts = [project_rows(piece, weights[0]) for piece in pieces]
    sides[0], acts, down_all = lax.optimization_barrier((sides[0], acts, down_all))
    fars = [
        [
            shift_chips(left[: left.shape[0] // 2], 1),
            shift_chips(right[right.shape[0] // 2 :], -1),
        ]
        for left, right in sides
    ]
    result = []
    for act, (left, right), far in zip(acts, sides, fars):
        act = act + project_rows(left, weights[1]) + project_rows(right, weights[3])
        act = act + jnp.concatenate([project_rows(part, weights[2]) for part in far], axis=0)
        hidden = hidden_of(act)
        hiddens = [hidden] + [shift_chips(hidden, k) for k in steps]
        result.append(dot(jnp.concatenate(hiddens, axis=1), down_all).astype(BF16))
    result = jnp.concatenate(result, axis=0)

    result, token_blocks = lax.optimization_barrier((result, token_blocks))
    returned = exchange(result)

    where = jnp.stack([chip, core]).astype(jnp.int32)
    mine = join_rows(token_blocks)
    keep, give = shared_terms(where, mine, swap_cores(mine), shared_gate, shared_up, shared_down)
    both = keep.astype(F32) + swap_cores(give).astype(F32)
    terms = jnp.split(both.astype(BF16), CHIPS)
    terms = [terms[0]] + [shift_chips(term, k) for term, k in zip(terms[1:], steps)]
    spread = jnp.where(hit, weight[:, None, :], 0.0).reshape(experts * half_cap, tok_rows)
    high = spread.astype(BF16)
    low = (spread - high.astype(F32)).astype(BF16)
    mine, theirs = combine(where, high, low, returned, terms)
    return (mine + swap_cores(theirs)).astype(BF16)


def solution(mesh):
    placed = (
        P("expert", "loop"),
        P("expert", None),
        P("expert", None),
        P("expert", "loop", None),
        P("expert", "loop", None),
        P("expert", "loop", None),
        P("loop", None),
        P("loop", None),
        P("loop", None),
    )
    return jax.shard_map(
        local, mesh=mesh, in_specs=placed, out_specs=P("expert", "loop"), check_vma=False
    )
```

```python
import jax
import jax.numpy as jnp
from jax import lax
from jax.experimental import pallas as pl
from jax.experimental.pallas import tpu as pltpu
from jax.sharding import PartitionSpec as P

CHIPS = 4
BF16 = jnp.bfloat16
F32 = jnp.float32


def swap_cores(value):
    return lax.ppermute(value, "loop", [(i, i ^ 1) for i in range(2 * CHIPS)])


def shift_chips(value, step):
    pairs = [
        (2 * chip + core, 2 * ((chip + step) % CHIPS) + core)
        for chip in range(CHIPS)
        for core in range(2)
    ]
    return lax.ppermute(value, "loop", pairs)


def dot(left, right):
    return jnp.dot(left, right, preferred_element_type=F32)


def project_rows(rows, weight):
    return lax.dot_general(rows, weight, (((1,), (1,)), ((), ())), preferred_element_type=F32)


def pick(chip, step, array, width):
    return lax.dynamic_slice_in_dim(array, ((chip - step) & (CHIPS - 1)) * width, width, axis=1)


def hidden_of(act):
    unit = act.shape[1] // 2
    return (jax.nn.silu(act[:, :unit]) * act[:, unit:]).astype(BF16)


def select_kernel(core_ref, tokens, other, chosen, out, half):
    first = core_ref[0] == 0
    whole = jnp.where(
        first,
        jnp.concatenate([tokens[...], other[...]], axis=1),
        jnp.concatenate([other[...], tokens[...]], axis=1),
    )
    out[...] = dot(chosen[...], whole).astype(BF16)
    rows = half.shape[0]
    half[...] = jnp.where(first, whole[:rows], whole[rows:])


def select_rows(core, tokens, other, chosen):
    rows, width = tokens.shape
    arrays = (tokens, other, chosen)
    shapes = [(chosen.shape[0], 2 * width), (rows // 2, 2 * width)]
    return pl.pallas_call(
        select_kernel,
        out_shape=[jax.ShapeDtypeStruct(shape, BF16) for shape in shapes],
        grid_spec=pltpu.PrefetchScalarGridSpec(
            num_scalar_prefetch=1,
            grid=(1,),
            in_specs=[pl.BlockSpec(array.shape, lambda k, c: (0, 0)) for array in arrays],
            out_specs=[pl.BlockSpec(shape, lambda k, c: (0, 0)) for shape in shapes],
        ),
        compiler_params=pltpu.CompilerParams(vmem_limit_bytes=24 << 20),
    )(core.reshape(1), *arrays)


def roll_kernel(chip_ref, *refs):
    out = refs[-1]
    unit = refs[0].shape[0]
    for i, ref in enumerate(refs[:-1]):
        out[0, i * unit : (i + 1) * unit, :] = ref[...]


def roll_features(chip, weights, width):
    unit = weights[0].shape[0]
    rows = unit * len(weights)
    return pl.pallas_call(
        roll_kernel,
        out_shape=jax.ShapeDtypeStruct((CHIPS, rows, width), BF16),
        grid_spec=pltpu.PrefetchScalarGridSpec(
            num_scalar_prefetch=1,
            grid=(CHIPS,),
            in_specs=[pl.BlockSpec((unit, width), lambda k, c: (0, (c[0] - k) & (CHIPS - 1)))]
            * len(weights),
            out_specs=pl.BlockSpec((1, rows, width), lambda k, c: (k, 0, 0)),
        ),
        compiler_params=pltpu.CompilerParams(vmem_limit_bytes=24 << 20),
    )(chip.reshape(1), *weights)


def near(k):
    return k ^ (k >> 1)


def pack_kernel(chip_ref, down, tokens, *outs):
    unit = down.shape[0]
    for index, out in enumerate(outs):

        @pl.when(pl.program_id(0) == index)
        def _(out=out):
            out[:unit, :] = down[...]
            out[unit:, :] = tokens[...]


def pack(chip, down, tokens):
    unit, (rows, width) = down.shape[0], tokens.shape
    shape = (unit + rows, width)
    return pl.pallas_call(
        pack_kernel,
        out_shape=[jax.ShapeDtypeStruct(shape, BF16)] * CHIPS,
        grid_spec=pltpu.PrefetchScalarGridSpec(
            num_scalar_prefetch=1,
            grid=(CHIPS,),
            in_specs=[
                pl.BlockSpec((unit, width), lambda k, c: (0, (c[0] + near(k)) & (CHIPS - 1))),
                pl.BlockSpec((rows, width), lambda k, c: (0, 0)),
            ],
            out_specs=[pl.BlockSpec(shape, lambda k, c: (0, 0))] * CHIPS,
        ),
        compiler_params=pltpu.CompilerParams(vmem_limit_bytes=24 << 20),
    )(chip.reshape(1), down, tokens)


def down_kernel(*refs):
    out = refs[-1]
    unit = out.shape[0] // (2 * CHIPS)
    for k, ref in enumerate(refs[:-1]):
        out[k * unit : (k + 1) * unit, :] = ref[:unit, :]


def join_down(unit, own, other):
    rows, width = own[0].shape
    tile = width // 2
    return pl.pallas_call(
        down_kernel,
        out_shape=jax.ShapeDtypeStruct((2 * CHIPS * unit, width), BF16),
        grid=(2,),
        in_specs=[pl.BlockSpec((rows, tile), lambda n: (0, n))] * (2 * CHIPS),
        out_specs=pl.BlockSpec((2 * CHIPS * unit, tile), lambda n: (0, n)),
        compiler_params=pltpu.CompilerParams(vmem_limit_bytes=24 << 20),
    )(*[part for pair in zip(own, other) for part in pair])


def act_of(gate, up):
    return (gate / (1.0 + jnp.exp(-gate)) * up).astype(BF16)


def shared_kernel(where_ref, *refs):
    mine, other, refs = refs[:CHIPS], refs[CHIPS : 2 * CHIPS], refs[2 * CHIPS :]
    gate, up, down, keep, give, gate_acc, up_acc, hidden = refs
    step = pl.program_id(0)
    rows = mine[0].shape[0]

    def pick_block(parts):
        block = parts[0][...]
        for k in range(1, CHIPS):
            block = jnp.where(step == k, parts[k][...], block)
        return block

    @pl.when(step < CHIPS)
    def _():
        block = jnp.concatenate([pick_block(mine), pick_block(other)], axis=0)
        first = step == 0
        gate_term, up_term = project_rows(block, gate[...]), project_rows(block, up[...])
        gate_acc[...] = jnp.where(first, gate_term, gate_acc[...] + gate_term)
        up_acc[...] = jnp.where(first, up_term, up_acc[...] + up_term)

    @pl.when(step == CHIPS - 1)
    def _():
        hidden[...] = act_of(gate_acc[...], up_acc[...])

    @pl.when(step >= CHIPS)
    def _():
        at = pl.ds(pl.multiple_of((step - CHIPS) * rows, rows), rows)
        term = dot(hidden[...], down[...]).astype(BF16)
        keep[at, :] = term[:rows]
        give[at, :] = term[rows:]


def shared_terms(where, mine, other, gate, up, down):
    unit = gate.shape[0]
    pack_rows, width = mine[0].shape
    half = pack_rows - unit
    rows = 2 * half
    shape = (CHIPS * half, width)
    whole = pl.BlockSpec(shape, lambda k, w: (0, 0))
    block = pl.BlockSpec((half, width), lambda k, w: (unit // half, 0))
    into = pl.BlockSpec(
        (unit, width), lambda k, w: (0, (w[0] - near(jnp.minimum(k, CHIPS - 1))) & (CHIPS - 1))
    )
    out_of = pl.BlockSpec(
        (unit, width), lambda k, w: (0, (w[0] + near(jnp.maximum(k - CHIPS, 0))) & (CHIPS - 1))
    )
    return pl.pallas_call(
        shared_kernel,
        out_shape=[jax.ShapeDtypeStruct(shape, BF16)] * 2,
        grid_spec=pltpu.PrefetchScalarGridSpec(
            num_scalar_prefetch=1,
            grid=(2 * CHIPS,),
            in_specs=[block] * (2 * CHIPS) + [into, into, out_of],
            out_specs=[whole] * 2,
            scratch_shapes=[
                pltpu.VMEM((rows, unit), F32),
                pltpu.VMEM((rows, unit), F32),
                pltpu.VMEM((rows, unit), BF16),
            ],
        ),
        compiler_params=pltpu.CompilerParams(vmem_limit_bytes=24 << 20),
    )(where, *mine, *other, gate, up, down)


def combine_kernel(where_ref, high, low, returned, *refs):
    shared, (mine, theirs) = refs[:CHIPS], refs[CHIPS:]
    contract = (((0,), (0,)), ((), ()))
    part = sum(ref[...].astype(F32) for ref in shared)
    none = jnp.zeros_like(part)
    total = jnp.where(
        where_ref[1] == 0,
        jnp.concatenate([part, none], axis=0),
        jnp.concatenate([none, part], axis=0),
    )
    for weight in (high, low):
        total = total + lax.dot_general(
            weight[...], returned[...], contract, preferred_element_type=F32
        )
    width = mine.shape[1]
    first = where_ref[1] == 0
    mine[...] = jnp.where(first, total[:, :width], total[:, width:])
    theirs[...] = jnp.where(first, total[:, width:], total[:, :width])


def combine(where, high, low, returned, shared):
    rows, width = high.shape[1], returned.shape[1]
    half = jax.ShapeDtypeStruct((rows, width // 2), F32)
    arrays = (high, low, returned, *shared)
    return pl.pallas_call(
        combine_kernel,
        out_shape=[half, half],
        grid_spec=pltpu.PrefetchScalarGridSpec(
            num_scalar_prefetch=1,
            grid=(1,),
            in_specs=[pl.BlockSpec(array.shape, lambda k, w: (0, 0)) for array in arrays],
            out_specs=[pl.BlockSpec(half.shape, lambda k, w: (0, 0))] * 2,
        ),
        compiler_params=pltpu.CompilerParams(vmem_limit_bytes=24 << 20),
    )(where, *arrays)


def local(tokens, routes, route_weights, gate_w, up_w, down_w, shared_gate, shared_up, shared_down):
    tok_rows, width = tokens.shape
    experts = lax.axis_size("expert")
    half_cap = tok_rows * routes.shape[1] * 4 // (3 * experts) // 2
    place = lax.axis_index("loop")
    chip, core = place >> 1, place & 1
    chip_width = 2 * width
    steps = (1, 3, 2)

    other_tokens = swap_cores(tokens)
    ids = jnp.arange(experts, dtype=jnp.int32)
    equal = routes.T[:, None, :] == ids[None, :, None]
    member = jnp.any(equal, axis=0)
    weight = jnp.sum(jnp.where(equal, route_weights.T[:, None, :], 0.0), axis=0)
    row = lax.broadcasted_iota(jnp.int32, (tok_rows, tok_rows), 0)
    col = lax.broadcasted_iota(jnp.int32, (tok_rows, tok_rows), 1)
    before = dot(member.astype(BF16), (row < col).astype(BF16)).astype(jnp.int32)
    slots = jnp.arange(half_cap, dtype=jnp.int32) + core * half_cap
    hit = member[:, None, :] & (before[:, None, :] == slots[None, :, None])
    selector = hit.astype(BF16).reshape(experts * half_cap, tok_rows)
    outgoing, sent_tokens = select_rows(core, tokens, other_tokens, selector)

    def exchange(value):
        value = value.reshape(experts, half_cap, chip_width)
        value = lax.all_to_all(value, "expert", split_axis=0, concat_axis=0, tiled=True)
        return value.reshape(experts * half_cap, chip_width)

    rows = exchange(outgoing)

    gate_own, up_own, down_mine, sent_tokens, _ = lax.optimization_barrier(
        (gate_w[0], up_w[0], down_w[0], sent_tokens, outgoing)
    )
    gate_other, up_other = swap_cores(gate_own), swap_cores(up_own)
    packs = pack(chip, down_mine, sent_tokens)
    packs = [packs[0]] + [shift_chips(part, k) for part, k in zip(packs[1:], steps)]
    weights = roll_features(chip, [gate_own, gate_other, up_own, up_other], chip_width)
    packs[1:3], weights = lax.optimization_barrier((packs[1:3], weights))
    own_pack, other_pack = packs, [swap_cores(part) for part in packs]
    rows, weights, own_pack, other_pack = lax.optimization_barrier(
        (rows, weights, own_pack, other_pack)
    )
    down_all = join_down(down_mine.shape[0], own_pack, other_pack)

    cut = rows.shape[0] // 2
    pieces = [rows[:cut], rows[cut:]]
    sides = [(shift_chips(piece, 1), shift_chips(piece, -1)) for piece in pieces]
    acts = [project_rows(piece, weights[0]) for piece in pieces]
    sides[0], acts, down_all = lax.optimization_barrier((sides[0], acts, down_all))
    fars = [
        [
            shift_chips(left[: left.shape[0] // 2], 1),
            shift_chips(right[right.shape[0] // 2 :], -1),
        ]
        for left, right in sides
    ]
    result = []
    for act, (left, right), far in zip(acts, sides, fars):
        act = act + project_rows(left, weights[1]) + project_rows(right, weights[3])
        act = act + jnp.concatenate([project_rows(part, weights[2]) for part in far], axis=0)
        hidden = hidden_of(act)
        if len(result) in (0, 1):
            left, right = shift_chips(hidden, 1), shift_chips(hidden, -1)
            middle = hidden.shape[0] // 2
            far = [shift_chips(left[:middle], 1), shift_chips(right[middle:], -1)]
            hiddens = [hidden, left, right, jnp.concatenate(far, axis=0)]
        else:
            hiddens = [hidden] + [shift_chips(hidden, k) for k in steps]
        result.append(dot(jnp.concatenate(hiddens, axis=1), down_all).astype(BF16))
    result = jnp.concatenate(result, axis=0)

    result, own_pack, other_pack = lax.optimization_barrier((result, own_pack, other_pack))
    returned = exchange(result)

    where = jnp.stack([chip, core]).astype(jnp.int32)
    keep, give = shared_terms(where, own_pack, other_pack, shared_gate, shared_up, shared_down)
    both = keep.astype(F32) + swap_cores(give).astype(F32)
    terms = jnp.split(both.astype(BF16), CHIPS)
    terms = [terms[0]] + [shift_chips(term, k) for term, k in zip(terms[1:], steps)]
    spread = jnp.where(hit, weight[:, None, :], 0.0).reshape(experts * half_cap, tok_rows)
    high = spread.astype(BF16)
    low = (spread - high.astype(F32)).astype(BF16)
    mine, theirs = combine(where, high, low, returned, terms)
    return (mine + swap_cores(theirs)).astype(BF16)


def solution(mesh):
    placed = (
        P("expert", "loop"),
        P("expert", None),
        P("expert", None),
        P("expert", "loop", None),
        P("expert", "loop", None),
        P("expert", "loop", None),
        P("loop", None),
        P("loop", None),
        P("loop", None),
    )
    return jax.shard_map(
        local, mesh=mesh, in_specs=placed, out_specs=P("expert", "loop"), check_vma=False
    )
```

```python
import jax
import jax.numpy as jnp
from jax import lax
from jax.experimental import pallas as pl
from jax.experimental.pallas import tpu as pltpu
from jax.sharding import PartitionSpec as P

CHIPS = 4
BF16 = jnp.bfloat16
F32 = jnp.float32


def swap_cores(value):
    return lax.ppermute(value, "loop", [(i, i ^ 1) for i in range(2 * CHIPS)])


def shift_chips(value, step):
    pairs = [
        (2 * chip + core, 2 * ((chip + step) % CHIPS) + core)
        for chip in range(CHIPS)
        for core in range(2)
    ]
    return lax.ppermute(value, "loop", pairs)


def dot(left, right):
    return jnp.dot(left, right, preferred_element_type=F32)


def project_rows(rows, weight):
    return lax.dot_general(rows, weight, (((1,), (1,)), ((), ())), preferred_element_type=F32)


def pick(chip, step, array, width):
    return lax.dynamic_slice_in_dim(array, ((chip - step) & (CHIPS - 1)) * width, width, axis=1)


def hidden_of(act):
    unit = act.shape[1] // 2
    return (jax.nn.silu(act[:, :unit]) * act[:, unit:]).astype(BF16)


def select_kernel(core_ref, tokens, other, chosen, out, half):
    first = core_ref[0] == 0
    whole = jnp.where(
        first,
        jnp.concatenate([tokens[...], other[...]], axis=1),
        jnp.concatenate([other[...], tokens[...]], axis=1),
    )
    out[...] = dot(chosen[...], whole).astype(BF16)
    rows = half.shape[0]
    half[...] = jnp.where(first, whole[:rows], whole[rows:])


def select_rows(core, tokens, other, chosen):
    rows, width = tokens.shape
    arrays = (tokens, other, chosen)
    shapes = [(chosen.shape[0], 2 * width), (rows // 2, 2 * width)]
    return pl.pallas_call(
        select_kernel,
        out_shape=[jax.ShapeDtypeStruct(shape, BF16) for shape in shapes],
        grid_spec=pltpu.PrefetchScalarGridSpec(
            num_scalar_prefetch=1,
            grid=(1,),
            in_specs=[pl.BlockSpec(array.shape, lambda k, c: (0, 0)) for array in arrays],
            out_specs=[pl.BlockSpec(shape, lambda k, c: (0, 0)) for shape in shapes],
        ),
        compiler_params=pltpu.CompilerParams(vmem_limit_bytes=24 << 20),
    )(core.reshape(1), *arrays)


def roll_kernel(chip_ref, *refs):
    out = refs[-1]
    unit = refs[0].shape[0]
    for i, ref in enumerate(refs[:-1]):
        out[0, i * unit : (i + 1) * unit, :] = ref[...]


def roll_features(chip, weights, width):
    unit = weights[0].shape[0]
    rows = unit * len(weights)
    return pl.pallas_call(
        roll_kernel,
        out_shape=jax.ShapeDtypeStruct((CHIPS, rows, width), BF16),
        grid_spec=pltpu.PrefetchScalarGridSpec(
            num_scalar_prefetch=1,
            grid=(CHIPS,),
            in_specs=[pl.BlockSpec((unit, width), lambda k, c: (0, (c[0] - k) & (CHIPS - 1)))]
            * len(weights),
            out_specs=pl.BlockSpec((1, rows, width), lambda k, c: (k, 0, 0)),
        ),
        compiler_params=pltpu.CompilerParams(vmem_limit_bytes=24 << 20),
    )(chip.reshape(1), *weights)


def near(k):
    return k ^ (k >> 1)


def pack_kernel(chip_ref, down, tokens, *outs):
    unit = down.shape[0]
    for index, out in enumerate(outs):

        @pl.when(pl.program_id(0) == index)
        def _(out=out):
            out[:unit, :] = down[...]
            out[unit:, :] = tokens[...]


def pack(chip, down, tokens):
    unit, (rows, width) = down.shape[0], tokens.shape
    shape = (unit + rows, width)
    return pl.pallas_call(
        pack_kernel,
        out_shape=[jax.ShapeDtypeStruct(shape, BF16)] * CHIPS,
        grid_spec=pltpu.PrefetchScalarGridSpec(
            num_scalar_prefetch=1,
            grid=(CHIPS,),
            in_specs=[
                pl.BlockSpec((unit, width), lambda k, c: (0, (c[0] + near(k)) & (CHIPS - 1))),
                pl.BlockSpec((rows, width), lambda k, c: (0, 0)),
            ],
            out_specs=[pl.BlockSpec(shape, lambda k, c: (0, 0))] * CHIPS,
        ),
        compiler_params=pltpu.CompilerParams(vmem_limit_bytes=24 << 20),
    )(chip.reshape(1), down, tokens)


def down_kernel(*refs):
    out = refs[-1]
    unit = out.shape[0] // (2 * CHIPS)
    for k, ref in enumerate(refs[:-1]):
        out[k * unit : (k + 1) * unit, :] = ref[:unit, :]


def join_down(unit, own, other):
    rows, width = own[0].shape
    tile = width // 2
    return pl.pallas_call(
        down_kernel,
        out_shape=jax.ShapeDtypeStruct((2 * CHIPS * unit, width), BF16),
        grid=(2,),
        in_specs=[pl.BlockSpec((rows, tile), lambda n: (0, n))] * (2 * CHIPS),
        out_specs=pl.BlockSpec((2 * CHIPS * unit, tile), lambda n: (0, n)),
        compiler_params=pltpu.CompilerParams(vmem_limit_bytes=24 << 20),
    )(*[part for pair in zip(own, other) for part in pair])


def split_kernel(rows, *outs):
    low = 0
    for out in outs:
        out[...] = rows[low : low + out.shape[0], :]
        low += out.shape[0]


def split_rows(rows):
    count, width = rows.shape
    tile = width // 2
    return pl.pallas_call(
        split_kernel,
        out_shape=[jax.ShapeDtypeStruct((count // 2, width), BF16)] * 2,
        grid=(2,),
        in_specs=[pl.BlockSpec((count, tile), lambda n: (0, n))],
        out_specs=[pl.BlockSpec((count // 2, tile), lambda n: (0, n))] * 2,
        compiler_params=pltpu.CompilerParams(vmem_limit_bytes=24 << 20),
    )(rows)


def act_of(gate, up):
    return (gate / (1.0 + jnp.exp(-gate)) * up).astype(BF16)


def shared_kernel(where_ref, *refs):
    mine, other, refs = refs[:CHIPS], refs[CHIPS : 2 * CHIPS], refs[2 * CHIPS :]
    gate, up, down, keep, give, gate_acc, up_acc, hidden = refs
    step = pl.program_id(0)
    rows = mine[0].shape[0]

    def pick_block(parts):
        block = parts[0][...]
        for k in range(1, CHIPS):
            block = jnp.where(step == k, parts[k][...], block)
        return block

    @pl.when(step < CHIPS)
    def _():
        block = jnp.concatenate([pick_block(mine), pick_block(other)], axis=0)
        first = step == 0
        gate_term, up_term = project_rows(block, gate[...]), project_rows(block, up[...])
        gate_acc[...] = jnp.where(first, gate_term, gate_acc[...] + gate_term)
        up_acc[...] = jnp.where(first, up_term, up_acc[...] + up_term)

    @pl.when(step == CHIPS - 1)
    def _():
        hidden[...] = act_of(gate_acc[...], up_acc[...])

    @pl.when(step >= CHIPS)
    def _():
        at = pl.ds(pl.multiple_of((step - CHIPS) * rows, rows), rows)
        term = dot(hidden[...], down[...]).astype(BF16)
        keep[at, :] = term[:rows]
        give[at, :] = term[rows:]


def shared_terms(where, mine, other, gate, up, down):
    unit = gate.shape[0]
    pack_rows, width = mine[0].shape
    half = pack_rows - unit
    rows = 2 * half
    shape = (CHIPS * half, width)
    whole = pl.BlockSpec(shape, lambda k, w: (0, 0))
    block = pl.BlockSpec((half, width), lambda k, w: (unit // half, 0))
    into = pl.BlockSpec(
        (unit, width), lambda k, w: (0, (w[0] - near(jnp.minimum(k, CHIPS - 1))) & (CHIPS - 1))
    )
    out_of = pl.BlockSpec(
        (unit, width), lambda k, w: (0, (w[0] + near(jnp.maximum(k - CHIPS, 0))) & (CHIPS - 1))
    )
    return pl.pallas_call(
        shared_kernel,
        out_shape=[jax.ShapeDtypeStruct(shape, BF16)] * 2,
        grid_spec=pltpu.PrefetchScalarGridSpec(
            num_scalar_prefetch=1,
            grid=(2 * CHIPS,),
            in_specs=[block] * (2 * CHIPS) + [into, into, out_of],
            out_specs=[whole] * 2,
            scratch_shapes=[
                pltpu.VMEM((rows, unit), F32),
                pltpu.VMEM((rows, unit), F32),
                pltpu.VMEM((rows, unit), BF16),
            ],
        ),
        compiler_params=pltpu.CompilerParams(vmem_limit_bytes=24 << 20),
    )(where, *mine, *other, gate, up, down)


def combine_kernel(where_ref, high, low, returned, *refs):
    shared, (mine, theirs) = refs[:CHIPS], refs[CHIPS:]
    contract = (((0,), (0,)), ((), ()))
    part = sum(ref[...].astype(F32) for ref in shared)
    none = jnp.zeros_like(part)
    total = jnp.where(
        where_ref[1] == 0,
        jnp.concatenate([part, none], axis=0),
        jnp.concatenate([none, part], axis=0),
    )
    for weight in (high, low):
        total = total + lax.dot_general(
            weight[...], returned[...], contract, preferred_element_type=F32
        )
    width = mine.shape[1]
    first = where_ref[1] == 0
    mine[...] = jnp.where(first, total[:, :width], total[:, width:])
    theirs[...] = jnp.where(first, total[:, width:], total[:, :width])


def combine(where, high, low, returned, shared):
    rows, width = high.shape[1], returned.shape[1]
    half = jax.ShapeDtypeStruct((rows, width // 2), F32)
    arrays = (high, low, returned, *shared)
    return pl.pallas_call(
        combine_kernel,
        out_shape=[half, half],
        grid_spec=pltpu.PrefetchScalarGridSpec(
            num_scalar_prefetch=1,
            grid=(1,),
            in_specs=[pl.BlockSpec(array.shape, lambda k, w: (0, 0)) for array in arrays],
            out_specs=[pl.BlockSpec(half.shape, lambda k, w: (0, 0))] * 2,
        ),
        compiler_params=pltpu.CompilerParams(vmem_limit_bytes=24 << 20),
    )(where, *arrays)


def local(tokens, routes, route_weights, gate_w, up_w, down_w, shared_gate, shared_up, shared_down):
    tok_rows, width = tokens.shape
    experts = lax.axis_size("expert")
    half_cap = tok_rows * routes.shape[1] * 4 // (3 * experts) // 2
    place = lax.axis_index("loop")
    chip, core = place >> 1, place & 1
    chip_width = 2 * width
    steps = (1, 3, 2)

    other_tokens = swap_cores(tokens)
    ids = jnp.arange(experts, dtype=jnp.int32)
    equal = routes.T[:, None, :] == ids[None, :, None]
    member = jnp.any(equal, axis=0)
    weight = jnp.sum(jnp.where(equal, route_weights.T[:, None, :], 0.0), axis=0)
    row = lax.broadcasted_iota(jnp.int32, (tok_rows, tok_rows), 0)
    col = lax.broadcasted_iota(jnp.int32, (tok_rows, tok_rows), 1)
    before = dot(member.astype(BF16), (row < col).astype(BF16)).astype(jnp.int32)
    slots = jnp.arange(half_cap, dtype=jnp.int32) + core * half_cap
    hit = member[:, None, :] & (before[:, None, :] == slots[None, :, None])
    selector = hit.astype(BF16).reshape(experts * half_cap, tok_rows)
    outgoing, sent_tokens = select_rows(core, tokens, other_tokens, selector)

    def exchange(value):
        value = value.reshape(experts, half_cap, chip_width)
        value = lax.all_to_all(value, "expert", split_axis=0, concat_axis=0, tiled=True)
        return value.reshape(experts * half_cap, chip_width)

    rows = exchange(outgoing)

    gate_own, up_own, down_mine, sent_tokens, _ = lax.optimization_barrier(
        (gate_w[0], up_w[0], down_w[0], sent_tokens, outgoing)
    )
    gate_other, up_other = swap_cores(gate_own), swap_cores(up_own)
    packs = pack(chip, down_mine, sent_tokens)
    packs = [packs[0]] + [shift_chips(part, k) for part, k in zip(packs[1:], steps)]
    weights = roll_features(chip, [gate_own, gate_other, up_own, up_other], chip_width)
    packs[1:3], weights = lax.optimization_barrier((packs[1:3], weights))
    own_pack, other_pack = packs, [swap_cores(part) for part in packs]
    rows, weights, own_pack, other_pack = lax.optimization_barrier(
        (rows, weights, own_pack, other_pack)
    )
    down_all = join_down(down_mine.shape[0], own_pack, other_pack)

    pieces = split_rows(rows)
    sides = [(shift_chips(piece, 1), shift_chips(piece, -1)) for piece in pieces]
    acts = [project_rows(piece, weights[0]) for piece in pieces]
    sides[0], acts, down_all = lax.optimization_barrier((sides[0], acts, down_all))
    fars = [
        [
            shift_chips(left[: left.shape[0] // 2], 1),
            shift_chips(right[right.shape[0] // 2 :], -1),
        ]
        for left, right in sides
    ]
    result = []
    for act, (left, right), far in zip(acts, sides, fars):
        act = act + project_rows(left, weights[1]) + project_rows(right, weights[3])
        act = act + jnp.concatenate([project_rows(part, weights[2]) for part in far], axis=0)
        hidden = hidden_of(act)
        if len(result) in (0, 1):
            left, right = shift_chips(hidden, 1), shift_chips(hidden, -1)
            middle = hidden.shape[0] // 2
            far = [shift_chips(left[:middle], 1), shift_chips(right[middle:], -1)]
            hiddens = [hidden, left, right, jnp.concatenate(far, axis=0)]
        else:
            hiddens = [hidden] + [shift_chips(hidden, k) for k in steps]
        result.append(dot(jnp.concatenate(hiddens, axis=1), down_all).astype(BF16))
    result = jnp.concatenate(result, axis=0)

    result, own_pack, other_pack = lax.optimization_barrier((result, own_pack, other_pack))
    returned = exchange(result)

    where = jnp.stack([chip, core]).astype(jnp.int32)
    keep, give = shared_terms(where, own_pack, other_pack, shared_gate, shared_up, shared_down)
    both = keep.astype(F32) + swap_cores(give).astype(F32)
    terms = jnp.split(both.astype(BF16), CHIPS)
    terms = [terms[0]] + [shift_chips(term, k) for term, k in zip(terms[1:], steps)]
    spread = jnp.where(hit, weight[:, None, :], 0.0).reshape(experts * half_cap, tok_rows)
    high = spread.astype(BF16)
    low = (spread - high.astype(F32)).astype(BF16)
    mine, theirs = combine(where, high, low, returned, terms)
    return (mine + swap_cores(theirs)).astype(BF16)


def solution(mesh):
    placed = (
        P("expert", "loop"),
        P("expert", None),
        P("expert", None),
        P("expert", "loop", None),
        P("expert", "loop", None),
        P("expert", "loop", None),
        P("loop", None),
        P("loop", None),
        P("loop", None),
    )
    return jax.shard_map(
        local, mesh=mesh, in_specs=placed, out_specs=P("expert", "loop"), check_vma=False
    )
```
